128 devices in a mesh: queue: 64 (over x, y, z_lo, core), tok: 2 (over z_hi).
Axes of the slice: x: 4, y: 4, z: 4 (z_hi: 2, z_lo: 2; z = z_hi * 2 + z_lo), core: 2. Of those that a mesh axis runs over, the one named last changes fastest.
Arguments:
- latents: bfloat16 [64, 512, 3072], P('queue', 'tok'), may hold values from -5 to 5
- levels: int32 [64], P('queue'), may hold values from 0 to 63, as said below
- offsets: int32 [64], P('queue'), may hold values from 0 to 7
- level_table: float32 [64, 3, 3072], replicated, may hold values from -3 to 3
- w_qkv: bfloat16 [3072, 3, 1536], P(None, None, 'tok'), may hold values from -0.07252963 to 0.07252963
- w_out: bfloat16 [1536, 3072], P('tok'), may hold values from -0.15625 to 0.15625
- head_scale: float32 [12], P('tok'), may hold values from 2 to 24
Outputs:
- updated: bfloat16 [64, 512, 3072], P('queue', 'tok')
The draws below stay inside these ranges and needn't reach their ends.
Inputs may be any that keep to these rules, and one draw needn't show every extreme that they name: levels never fall from one frame to the next; frame f has a level from f * 1 to f * 1 + max(1, 1); the first frame has level 0 and the last 63.
All inputs are finite; a program needn't handle non-finite values.
Results may differ from the reference program's by a relative error of at most 0.01.
Values may be sent and summed in bfloat16 or wider, within the bound.
A program may use at most 192 MiB of HBM per device.

```python
import math
import jax
import jax.numpy as jnp
from jax import lax

D = 3072
HEADS = 12
DH = 128
WIN = 8
LEVELS = 64
FRAME_TOK = 512
FRAMES = 64


def draw_levels(key, part):
    key = jax.random.fold_in(key, 11)
    base = jnp.arange(FRAMES, dtype=jnp.int32) * LEVELS // FRAMES
    jitter = jax.random.randint(key, (FRAMES,), 0, max(LEVELS // FRAMES, 1) + 1, dtype=jnp.int32)
    stepped = jnp.minimum(base + jitter, LEVELS - 1)
    stepped = stepped.at[0].set(0)
    stepped = lax.cummax(stepped, axis=0)
    stepped = stepped.at[FRAMES - 1].set(LEVELS - 1)
    return stepped.astype(jnp.int32)


def draw_latents(key, part):
    key = jax.random.fold_in(key, 41)
    first_key = jax.random.fold_in(key, 0)
    proto_key = jax.random.fold_in(key, 2)
    member_key = jax.random.fold_in(key, 3)
    members = jax.random.randint(member_key, (FRAMES, FRAME_TOK), 0, 8, dtype=jnp.int32)
    frame_rows = jnp.arange(FRAMES, dtype=jnp.int32)[:, None]
    protos = jax.random.truncated_normal(proto_key, -3.5, 3.5, (FRAMES, 8, D), jnp.float32)
    noise = jax.random.truncated_normal(first_key, -3.5, 3.5, (FRAMES, FRAME_TOK, D), jnp.float32)
    values = 0.85 * protos[frame_rows, members] + 0.55 * noise
    return values.astype(jnp.bfloat16)


def draw_w_qkv(key, part):
    key = jax.random.fold_in(key, 21)
    query_key, key_key, value_key = jax.random.split(key, 3)
    factor = D ** (-0.5)
    query_part = jax.random.truncated_normal(query_key, -4.0, 4.0, (D, HEADS * DH), jnp.float32) * factor
    key_part = jax.random.truncated_normal(key_key, -4.0, 4.0, (D, HEADS * DH), jnp.float32) * factor
    value_part = jax.random.truncated_normal(value_key, -4.0, 4.0, (D, HEADS * DH), jnp.float32) * factor
    return jnp.stack([query_part, key_part, value_part], axis=1).astype(jnp.bfloat16)


def draw_head_scale(key, part):
    key = jax.random.fold_in(key, 31)
    spread_key, top_key, low_key = jax.random.split(key, 3)
    logs = jax.random.uniform(spread_key, (HEADS,), jnp.float32, math.log(2.0), math.log(24.0))
    values = jnp.exp(logs)
    top_head = jax.random.randint(top_key, (), 0, HEADS, dtype=jnp.int32)
    low_head = (top_head + 1 + jax.random.randint(low_key, (), 0, HEADS - 1, dtype=jnp.int32)) % HEADS
    heads = jnp.arange(HEADS, dtype=jnp.int32)
    values = jnp.where(heads == top_head, jnp.float32(24.0), values)
    values = jnp.where(heads == low_head, jnp.float32(2.0), values)
    return values.astype(jnp.float32)


def touch_ends(drawn, stream_key, low, largest):
    shape = drawn.shape
    spot = [jax.random.randint(jax.random.fold_in(stream_key, axis), (), 0, shape[axis]) for axis in range(len(shape))]
    drawn = drawn.at[tuple(spot)].set(low)
    longest = shape.index(max(shape))
    spot[longest] = (spot[longest] + 1) % shape[longest]
    return drawn.at[tuple(spot)].set(largest)


def level_of(own_key, extent, pieces, least, largest):
    def one(dim, shards_of):
        draws = jax.random.uniform(jax.random.fold_in(jax.random.fold_in(own_key, 6), dim), (shards_of,), jnp.float32, least / len(pieces), largest / len(pieces))
        return jnp.repeat(jnp.exp(draws), extent[dim] // shards_of).reshape((-1,) + (1,) * (len(extent) - dim - 1))

    factor_of = one(*pieces[0])
    for cut in pieces[1:]:
        factor_of = factor_of * one(*cut)
    return factor_of


def normal_values(stream_key, shape, scale, reach, pieces=(), held_as=jnp.bfloat16):
    values = jax.random.normal(stream_key, shape, jnp.float32) * scale
    if len(pieces) > 0:
        values = level_of(stream_key, shape, pieces, -0.22, 0.18) * values
    return jnp.clip(values, min=-reach, max=reach).astype(held_as)


def setup_inputs(seed: int = 0) -> dict:
    splits = jax.random.split(jax.random.key(seed), 8)
    latents = draw_latents(jax.random.fold_in(splits[7], 71), 0)
    levels = draw_levels(jax.random.fold_in(splits[7], 71), 0)
    offsets = touch_ends(jax.random.randint(splits[2], (FRAMES,), 0, WIN), jax.random.fold_in(splits[2], 1), 0, WIN - 1).astype(jnp.int32)
    level_table = normal_values(splits[3], (LEVELS, 3, D), 0.5, 3.0, (), jnp.float32)
    w_qkv = draw_w_qkv(jax.random.fold_in(splits[7], 71), 0)
    w_out = normal_values(splits[5], (HEADS * DH, D), (HEADS * DH) ** -0.5, 0.15625, ((0, 2),))
    head_scale = draw_head_scale(jax.random.fold_in(splits[7], 71), 0)
    return {"latents": latents, "levels": levels, "offsets": offsets, "level_table": level_table, "w_qkv": w_qkv, "w_out": w_out, "head_scale": head_scale}


epsilon = 1e-06

def rms_rows(values):
    return values * lax.rsqrt(lax.optimization_barrier(jnp.mean(values * values, axis=-1, keepdims=True)) + epsilon)

def attend_head(query_head, key_head, value_head, key_valid):
    scores = jnp.dot(query_head, key_head.T, preferred_element_type=jnp.float32)
    scores = jnp.where(key_valid[None, :], scores, -1e+30)
    row_peak = lax.optimization_barrier(jnp.max(scores, axis=1, keepdims=True))
    weights = jnp.exp(scores - row_peak)
    row_total = lax.optimization_barrier(jnp.sum(weights, axis=1, keepdims=True))
    weighted = jnp.dot(weights.astype(jnp.bfloat16), value_head, preferred_element_type=jnp.float32)
    return weighted / row_total

def window_attention(query_rows, key_window, value_window, key_valid):

    def one_head(operands):
        return attend_head(operands[0], operands[1], operands[2], key_valid)
    result = lax.map(one_head, (jnp.moveaxis(query_rows, 1, 0), jnp.moveaxis(key_window, 1, 0), jnp.moveaxis(value_window, 1, 0)))
    result = jnp.moveaxis(result, 0, 1)
    return result.reshape(result.shape[0], -1).astype(jnp.bfloat16)

def reference(latents, levels, offsets, level_table, w_qkv, w_out, head_scale):
    frames, frame_tok, width = latents.shape
    modulation = level_table[levels]
    latent_f = latents.astype(jnp.float32)
    normed = (rms_rows(latent_f) * (1.0 + modulation[:, 1][:, None, :]) + modulation[:, 0][:, None, :]).astype(jnp.bfloat16)
    proj = jnp.dot(normed.reshape(-1, width), w_qkv.reshape(width, -1), preferred_element_type=jnp.float32)
    proj = proj.reshape(frames, frame_tok, 3, HEADS, DH)
    queries = (rms_rows(proj[:, :, 0]) * head_scale[:, None] / jnp.sqrt(jnp.float32(DH))).astype(jnp.bfloat16)
    key_rows = rms_rows(proj[:, :, 1]).astype(jnp.bfloat16)
    value_rows = proj[:, :, 2].astype(jnp.bfloat16)
    margin = WIN - 1
    key_pad = jnp.pad(key_rows, ((margin, margin), (0, 0), (0, 0), (0, 0)))
    value_pad = jnp.pad(value_rows, ((margin, margin), (0, 0), (0, 0), (0, 0)))

    def one_frame(frame_index):
        first = (frame_index - offsets[frame_index]).astype(jnp.int32)
        key_window = lax.dynamic_slice_in_dim(key_pad, first + margin, WIN, 0).reshape(WIN * frame_tok, HEADS, DH)
        value_window = lax.dynamic_slice_in_dim(value_pad, first + margin, WIN, 0).reshape(WIN * frame_tok, HEADS, DH)
        source = first + jnp.arange(WIN, dtype=jnp.int32)
        valid = (source >= 0) & (source < frames)
        key_valid = jnp.repeat(valid, frame_tok)
        return window_attention(queries[frame_index], key_window, value_window, key_valid)
    attended = lax.map(one_frame, jnp.arange(frames, dtype=jnp.int32))
    branch = jnp.dot(attended.reshape(frames * frame_tok, -1), w_out, preferred_element_type=jnp.float32)
    branch = branch.reshape(frames, frame_tok, width)
    return (latent_f + modulation[:, 2][:, None, :] * branch).astype(jnp.bfloat16)
```

```python
import functools

import jax
import jax.numpy as jnp
from jax import lax
from jax.experimental import pallas as pl
from jax.experimental.pallas import tpu as pltpu
from jax.sharding import PartitionSpec as P

D = 3072
DH = 128
WIN = 8
TOK = 512
HALF = 256
TRI = 384
COLS = 16
EPS = 1e-6
LOW = -1e30
HIGH = 1e30
WSUB = 4
MESH = pl.DeviceIdType.MESH
UP, DOWN = 0, 1
A, B, C1, D1, C2, D2 = range(6)


def body(
    x_ref, mod_ref, w_hbm, wo_hbm, off_ref, hs_ref,
    out_ref,
    near, far, qb, w_v, wo_v, nrm, st_kv, st_q, scores, acc_s, m_s, l_s, att, ob, offs,
    w_sem, off_sem, cut_s, cut_r, inkv_s, inkv_r, inq_s, inq_r, y_s, y_r, f_s, f_r,
    c0_s, c0_r, c1_s, c1_r, c2_s, c2_r, wc_s, wc_r, wi_s, wi_r, wk_s, wk_r, wj_s, wj_r, o_s, o_r,
):
    q = lax.axis_index("queue")
    t = lax.axis_index("tok")
    core = lax.rem(q, 2)
    zlo = lax.rem(q // 2, 2)
    col = q // 4
    inner_q = q + 2 - 4 * zlo
    inner = (inner_q, t)
    cut = (inner_q, 1 - t)
    peer = (q, 1 - t)
    other = (q + 1 - 2 * core, t)
    upper = (q + 4, t)
    lower = (q - 4, t)
    has_up, has_low = col < COLS - 1, col > 0
    pending = []

    def send(src, dst, s_sem, r_sem, to, when=None):
        copy = pltpu.make_async_remote_copy(
            src_ref=src, dst_ref=dst, send_sem=s_sem, recv_sem=r_sem, device_id=to, device_id_type=MESH
        )
        pending.append((copy, when))
        if when is None:
            copy.start()
        else:
            pl.when(when)(copy.start)

    def recv(dst, s_sem, r_sem, to, when=None):
        copy = pltpu.make_async_remote_copy(
            src_ref=dst, dst_ref=dst, send_sem=s_sem, recv_sem=r_sem, device_id=to, device_id_type=MESH
        )
        if when is None:
            copy.wait_recv()
        else:
            pl.when(when)(copy.wait_recv)

    loads = [
        pltpu.make_async_copy(w_hbm.at[i], w_v.at[i], w_sem.at[i]) for i in range(3)
    ]
    for i in (1, 2, 0):
        loads[i].start()
    wo_load = pltpu.make_async_copy(
        wo_hbm, wo_v.at[pl.ds(pl.multiple_of(t * 768, 768), 768)], w_sem.at[3]
    )
    wo_load.start()

    barrier = pltpu.get_barrier_semaphore()
    for to in (inner, cut, peer, other):
        pl.semaphore_signal(barrier, inc=1, device_id=to, device_id_type=MESH)

    @pl.when(has_up)
    def _():
        pl.semaphore_signal(barrier, inc=1, device_id=upper, device_id_type=MESH)

    @pl.when(has_low)
    def _():
        pl.semaphore_signal(barrier, inc=1, device_id=lower, device_id_type=MESH)

    def normalize(r):
        rows = pl.ds(r * 128, 128)
        x = x_ref[0, rows, :].astype(jnp.float32)
        inv = lax.rsqrt(jnp.mean(x * x, axis=-1, keepdims=True) + EPS)
        nrm[0, rows, :] = (x * inv * (1.0 + mod_ref[1:2, :]) + mod_ref[0:1, :]).astype(jnp.bfloat16)

    def send_normed(r):
        rows = pl.ds(r * 128, 128)
        send(nrm.at[0, rows], nrm.at[1, rows], cut_s.at[r], cut_r.at[r], cut)

    normalize(0)
    pl.semaphore_wait(barrier, 4 + jnp.where(has_up, 1, 0) + jnp.where(has_low, 1, 0))
    send_normed(0)
    normalize(1)
    send_normed(1)
    send(off_ref, offs, off_sem.at[0], off_sem.at[1], inner)

    slot_of = {A: zlo, B: 1 - zlo, C1: 1 - zlo, D1: zlo, C2: 1 - zlo, D2: zlo}
    own0 = pl.multiple_of(t * HALF, HALF)
    frn0 = pl.multiple_of((1 - t) * HALF, HALF)
    rows_of = {
        A: pl.ds(own0, 256), B: pl.ds(own0, 256),
        C1: pl.ds(frn0, 128), D1: pl.ds(frn0, 128),
        C2: pl.ds(pl.multiple_of(frn0 + 128, 128), 128), D2: pl.ds(pl.multiple_of(frn0 + 128, 128), 128),
    }

    def frame(piece, of_core=core):
        return of_core + 2 * slot_of[piece]

    def near_at(side, piece, of_core=core):
        return near.at[side, frame(piece, of_core), :, rows_of[piece], :]

    def far_at(side, piece, of_core=core):
        return far.at[side, frame(piece, of_core), :, rows_of[piece], :]

    def project(part, nslot, src0, rows, piece):
        st_rows = pl.ds((0, 256, 384)[part], rows)
        for mat in (1, 2, 0):
            if part == 0:
                loads[mat].wait()
            y = jnp.dot(
                nrm[nslot, src0 : src0 + rows, :], w_v[mat], preferred_element_type=jnp.float32
            )
            thirds = []
            for h in range(6):
                yh = y[:, h * DH : (h + 1) * DH]
                if mat != 2:
                    yh = yh * lax.rsqrt(jnp.mean(yh * yh, axis=-1, keepdims=True) + EPS)
                if mat == 0:
                    yh = yh * hs_ref[h] * (DH ** -0.5)
                thirds.append(yh.astype(jnp.bfloat16))
            for h in range(3):
                lanes = slice(h * DH, (h + 1) * DH)
                mine = jnp.where(zlo == 0, thirds[h], thirds[h + 3])
                theirs = jnp.where(zlo == 0, thirds[h + 3], thirds[h])
                if mat == 0:
                    qb[slot_of[piece], rows_of[piece], lanes] = mine
                    st_q[st_rows, lanes] = theirs
                else:
                    far[0, frame(piece), mat - 1, rows_of[piece], lanes] = mine
                    st_kv[mat - 1, st_rows, lanes] = theirs
            if mat == 2:
                send(st_kv.at[:, st_rows], far_at(0, piece), inkv_s.at[part], inkv_r.at[part], inner)
                spread(piece)
            if mat == 0:
                send(
                    st_q.at[st_rows], qb.at[slot_of[piece], rows_of[piece]],
                    inq_s.at[part], inq_r.at[part], inner,
                )

    def spread(piece):
        send(far_at(0, piece), near_at(1, piece), y_s.at[UP, piece], y_r.at[UP, piece], upper, has_up)
        send(far_at(0, piece), near_at(0, piece), y_s.at[DOWN, piece], y_r.at[DOWN, piece], lower, has_low)
        send(far_at(0, piece), far_at(0, piece), c0_s.at[piece], c0_r.at[piece], other)

    def from_inner(part, piece):
        recv(far_at(0, piece), inkv_s.at[part], inkv_r.at[part], inner)
        spread(piece)

    def pass_on(piece):
        recv(near_at(1, piece), y_s.at[UP, piece], y_r.at[UP, piece], upper, has_low)
        send(
            near_at(1, piece), far_at(2, piece), f_s.at[UP, piece], f_r.at[UP, piece], upper,
            has_up & has_low & (frame(piece) >= 1),
        )
        send(near_at(1, piece), near_at(1, piece), c1_s.at[UP, piece], c1_r.at[UP, piece], other, has_low)
        recv(near_at(0, piece), y_s.at[DOWN, piece], y_r.at[DOWN, piece], lower, has_up)
        send(
            near_at(0, piece), far_at(1, piece), f_s.at[DOWN, piece], f_r.at[DOWN, piece], lower,
            has_up & has_low & (frame(piece) <= 2),
        )
        send(near_at(0, piece), near_at(0, piece), c1_s.at[DOWN, piece], c1_r.at[DOWN, piece], other, has_up)

    from_up2, from_low2 = col < COLS - 2, col > 1

    def share_far(piece):
        when = from_low2 & (frame(piece) >= 1)
        recv(far_at(2, piece), f_s.at[UP, piece], f_r.at[UP, piece], upper, when)
        send(far_at(2, piece), far_at(2, piece), c2_s.at[UP, piece], c2_r.at[UP, piece], other, when)
        when = from_up2 & (frame(piece) <= 2)
        recv(far_at(1, piece), f_s.at[DOWN, piece], f_r.at[DOWN, piece], lower, when)
        send(far_at(1, piece), far_at(1, piece), c2_s.at[DOWN, piece], c2_r.at[DOWN, piece], other, when)

    j = core + 2 * zlo
    w_rows = 192 // WSUB

    def quarter(half, which, sub):
        return pl.ds(pl.multiple_of(half * 768 + which * 192 + sub * w_rows, 16), w_rows)

    other_j, inner_j = j + 1 - 2 * core, j + 2 - 4 * zlo
    diag_j = 3 - j

    def wo_cut(sub):
        src = pl.ds(pl.multiple_of(inner_j * 192 + sub * w_rows, 16), w_rows)
        send(wo_hbm.at[src], wo_v.at[quarter(t, inner_j, sub)], wc_s.at[sub], wc_r.at[sub], cut)

    def wo_share(sub):
        mine = wo_v.at[quarter(1 - t, j, sub)]
        recv(mine, wc_s.at[sub], wc_r.at[sub], cut)
        send(mine, mine, wi_s.at[sub], wi_r.at[sub], inner)
        send(mine, mine, wk_s.at[sub], wk_r.at[sub], other)

    def wo_second(sub):
        theirs = wo_v.at[quarter(1 - t, inner_j, sub)]
        recv(theirs, wi_s.at[sub], wi_r.at[sub], inner)
        send(theirs, theirs, wj_s.at[sub], wj_r.at[sub], other)

    def wo_last(sub):
        recv(wo_v.at[quarter(1 - t, other_j, sub)], wk_s.at[sub], wk_r.at[sub], other)
        recv(wo_v.at[quarter(1 - t, diag_j, sub)], wj_s.at[sub], wj_r.at[sub], other)

    project(0, 0, 0, 256, A)

    @pl.when(col == COLS - 1)
    def _():
        near[0] = jnp.zeros_like(near[0])

    @pl.when(col == 0)
    def _():
        near[1] = jnp.zeros_like(near[1])

    @pl.when(col >= COLS - 2)
    def _():
        far[1] = jnp.zeros_like(far[1])

    @pl.when(col <= 1)
    def _():
        far[2] = jnp.zeros_like(far[2])

    from_inner(0, B)
    pass_on(A)
    recv(nrm.at[1, pl.ds(0, 128)], cut_s.at[0], cut_r.at[0], cut)
    project(1, 1, 0, 128, C1)
    pass_on(B)
    from_inner(1, D1)
    recv(nrm.at[1, pl.ds(128, 128)], cut_s.at[1], cut_r.at[1], cut)
    for sub in range(WSUB):
        wo_cut(sub)
    project(2, 1, 128, 128, C2)
    pass_on(C1)
    pass_on(D1)
    from_inner(2, D2)
    wo_share(0)
    pass_on(C2)
    pass_on(D2)
    wo_share(1)

    recv(offs, off_sem.at[0], off_sem.at[1], inner)
    for part, piece in ((0, B), (1, D1), (2, D2)):
        recv(qb.at[slot_of[piece], rows_of[piece]], inq_s.at[part], inq_r.at[part], inner)
    for piece in range(6):
        recv(near_at(1, piece, 1 - core), c1_s.at[UP, piece], c1_r.at[UP, piece], other, has_low)
        recv(near_at(0, piece, 1 - core), c1_s.at[DOWN, piece], c1_r.at[DOWN, piece], other, has_up)

    def offset_of(slot):
        return jnp.where(slot == zlo, off_ref[0], offs[0])

    def attend(slot, half, h, blocks, first):
        lanes = pl.ds(pl.multiple_of(h * DH, DH), DH)
        rows = pl.ds(pl.multiple_of(half * HALF, HALF), HALF)
        place = (slot * 2 + half) * 3 + h
        queries = qb[slot, rows, lanes]
        peak = None
        for b, (ref, lead, valid) in enumerate(blocks):
            keys = ref[(*lead, 0, slice(None), lanes)]
            s = lax.dot_general(
                queries, keys, (((1,), (1,)), ((), ())), preferred_element_type=jnp.float32
            )
            scores[:, b * TOK : (b + 1) * TOK] = s
            top = jnp.max(s, axis=1, keepdims=True)
            if valid is not None:
                top = jnp.where(valid, top, LOW)
            peak = top if peak is None else jnp.maximum(peak, top)
        if not first:
            before = m_s[place][:, :1]
            peak = jnp.maximum(peak, before)
        total = None
        weighted = None
        for b, (ref, lead, valid) in enumerate(blocks):
            base = peak if valid is None else jnp.where(valid, peak, HIGH)
            p = jnp.exp(scores[:, b * TOK : (b + 1) * TOK] - base)
            part = jnp.sum(p, axis=1, keepdims=True)
            values = ref[(*lead, 1, slice(None), lanes)]
            o = jnp.dot(p.astype(jnp.bfloat16), values, preferred_element_type=jnp.float32)
            total = part if total is None else total + part
            weighted = o if weighted is None else weighted + o
        if first:
            m_s[place] = jnp.broadcast_to(peak, (HALF, DH))
            l_s[place] = jnp.broadcast_to(total, (HALF, DH))
            acc_s[place] = weighted
        else:
            scale = jnp.exp(before - peak)
            total = total + l_s[place][:, :1] * scale
            weighted = weighted + acc_s[place] * scale
            ob[slot, rows, lanes] = (weighted / total).astype(jnp.bfloat16)

    def stage_near(slot, half, h):
        mine = core + 2 * slot
        o = offset_of(slot)
        blocks = [(far, (0, mine), None)]
        for i in range(4):
            below = 4 + i - mine > WIN - 1 - o
            side = jnp.where(below, 1, 0)
            valid = jnp.where(below, has_low, has_up)
            blocks.append((near, (side, i), valid))
        attend(slot, half, h, blocks, True)

    def stage_far(slot, half, h):
        mine = core + 2 * slot
        o = offset_of(slot)
        blocks = []
        for n in range(3):
            r = n + jnp.where(n >= mine, 1, 0)
            less = r < mine
            inside = jnp.where(less, mine - r <= o, r - mine <= WIN - 1 - o)
            side = jnp.where(inside, 0, jnp.where(less, 1, 2))
            valid = inside | jnp.where(less, from_up2, from_low2)
            blocks.append((far, (side, r), valid))
        attend(slot, half, h, blocks, False)

    def near_loop(i, carry):
        stage_near(i // 6, lax.rem(i // 3, 2), lax.rem(i, 3))
        return carry

    lax.fori_loop(0, 6, near_loop, 0)
    wo_share(2)
    wo_second(0)
    lax.fori_loop(6, 12, near_loop, 0)
    wo_share(3)
    wo_second(1)

    for piece in range(6):
        share_far(piece)
    wo_second(2)
    wo_second(3)
    for piece in range(6):
        recv(far_at(0, piece, 1 - core), c0_s.at[piece], c0_r.at[piece], other)
        recv(
            far_at(2, piece, 1 - core), c2_s.at[UP, piece], c2_r.at[UP, piece], other,
            from_low2 & (frame(piece, 1 - core) >= 1),
        )
        recv(
            far_at(1, piece, 1 - core), c2_s.at[DOWN, piece], c2_r.at[DOWN, piece], other,
            from_up2 & (frame(piece, 1 - core) <= 2),
        )

    def att_at(triple):
        return att.at[:, pl.ds(pl.multiple_of(triple * TRI, 128), TRI)]

    triple = 2 * t + zlo
    for n, (slot, half, to) in enumerate(
        ((1 - zlo, 1 - t, cut), (1 - zlo, t, inner), (zlo, 1 - t, peer), (zlo, t, None))
    ):
        lax.fori_loop(0, 3, lambda h, carry: (stage_far(slot, half, h), carry)[1], 0)
        rows = pl.ds(pl.multiple_of(half * HALF, HALF), HALF)
        if to is None:
            for h in range(3):
                att[:, pl.ds(pl.multiple_of(triple * TRI + h * DH, 128), DH)] = ob[slot, rows, h * DH : (h + 1) * DH]
        else:
            send(ob.at[slot, rows], att_at(triple), o_s.at[n], o_r.at[n], to)

    wo_load.wait()
    for sub in range(WSUB):
        wo_last(sub)
    for n, (from_t, from_z, to) in enumerate(((1 - t, 1 - zlo, cut), (t, 1 - zlo, inner), (1 - t, zlo, peer))):
        recv(att_at(2 * from_t + from_z), o_s.at[n], o_r.at[n], to)

    def out_tile(n, carry):
        lanes = pl.ds(pl.multiple_of(n * 512, 512), 512)
        branch = jnp.dot(att[...], wo_v[:, lanes], preferred_element_type=jnp.float32)
        x = x_ref[0, :, lanes].astype(jnp.float32)
        out_ref[0, :, lanes] = (x + mod_ref[2:3, lanes] * branch).astype(jnp.bfloat16)
        return carry

    lax.fori_loop(0, D // 512, out_tile, 0)
    for copy, when in pending:
        if when is None:
            copy.wait_send()
        else:
            pl.when(when)(copy.wait_send)


def shards(latents, levels, offsets, level_table, w_qkv, w_out, head_scale):
    table = jnp.transpose(level_table, (1, 0, 2))
    modulation = lax.dynamic_index_in_dim(table, levels[0], 1, keepdims=False)
    weights = jnp.transpose(w_qkv, (1, 0, 2))
    bf, f32 = jnp.bfloat16, jnp.float32
    dma = pltpu.SemaphoreType.DMA
    vmem = pl.BlockSpec(memory_space=pltpu.VMEM)
    smem = pl.BlockSpec(memory_space=pltpu.SMEM)
    hbm = pl.BlockSpec(memory_space=pl.ANY)
    pair = lambda *n: [dma(n), dma(n)]
    return pl.pallas_call(
        body,
        out_shape=jax.ShapeDtypeStruct((1, HALF, D), bf),
        in_specs=[vmem, vmem, hbm, hbm, smem, smem],
        out_specs=vmem,
        scratch_shapes=[
            pltpu.VMEM((2, 4, 2, TOK, TRI), bf),
            pltpu.VMEM((3, 4, 2, TOK, TRI), bf),
            pltpu.VMEM((2, TOK, TRI), bf),
            pltpu.VMEM((3, D, 768), bf),
            pltpu.VMEM((1536, D), bf),
            pltpu.VMEM((2, HALF, D), bf),
            pltpu.VMEM((2, TOK, TRI), bf),
            pltpu.VMEM((TOK, TRI), bf),
            pltpu.VMEM((HALF, 5 * TOK), f32),
            pltpu.VMEM((12, HALF, DH), f32),
            pltpu.VMEM((12, HALF, DH), f32),
            pltpu.VMEM((12, HALF, DH), f32),
            pltpu.VMEM((HALF, 1536), bf),
            pltpu.VMEM((2, TOK, TRI), bf),
            pltpu.SMEM((1,), jnp.int32),
            dma((4,)), dma((2,)),
            *pair(2), *pair(3), *pair(3), *pair(2, 6), *pair(2, 6),
            *pair(6), *pair(2, 6), *pair(2, 6),
            *pair(WSUB), *pair(WSUB), *pair(WSUB), *pair(WSUB), *pair(3),
        ],
        compiler_params=pltpu.CompilerParams(
            collective_id=0, has_side_effects=True, vmem_limit_bytes=62 * 2**20
        ),
        cost_estimate=pl.CostEstimate(flops=17 * 10**9, bytes_accessed=25 * 10**6, transcendentals=13 * 10**6),
        name="frame_attention",
    )(latents, modulation, weights, w_out, offsets, head_scale)


def solution(mesh):
    placed = (
        P("queue", "tok", None),
        P("queue"),
        P("queue"),
        P(),
        P(None, None, "tok"),
        P("tok", None),
        P("tok"),
    )
    return jax.shard_map(
        shards, mesh=mesh, in_specs=placed, out_specs=P("queue", "tok", None), check_vma=False
    )
```

```python
import functools

import jax
import jax.numpy as jnp
from jax import lax
from jax.experimental import pallas as pl
from jax.experimental.pallas import tpu as pltpu
from jax.sharding import PartitionSpec as P

D = 3072
DH = 128
WIN = 8
TOK = 512
HALF = 256
TRI = 384
COLS = 16
EPS = 1e-6
LOW = -1e30
HIGH = 1e30
WSUB = 4
MESH = pl.DeviceIdType.MESH
UP, DOWN = 0, 1
A, B, C1, D1, C2, D2 = range(6)


def body(
    x_ref, mod_ref, w_hbm, wo_hbm, off_ref, hs_ref,
    out_ref,
    near_a, near_c, far_a, far_c, qb, w_v, wo_v, nrm, st_kv, st_q, even, odd, acc_s, m_s, l_s, att, ob, offs,
    w_sem, off_sem, cut_s, cut_r, inkv_s, inkv_r, inq_s, inq_r, y_s, y_r, f_s, f_r,
    c0_s, c0_r, c1_s, c1_r, c2_s, c2_r, wc_s, wc_r, wi_s, wi_r, wk_s, wk_r, wj_s, wj_r, o_s, o_r,
):
    q = lax.axis_index("queue")
    t = lax.axis_index("tok")
    core = lax.rem(q, 2)
    zlo = lax.rem(q // 2, 2)
    col = q // 4
    inner_q = q + 2 - 4 * zlo
    inner = (inner_q, t)
    cut = (inner_q, 1 - t)
    peer = (q, 1 - t)
    other = (q + 1 - 2 * core, t)
    upper = (q + 4, t)
    lower = (q - 4, t)
    has_up, has_low = col < COLS - 1, col > 0
    pending = []

    def send(src, dst, s_sem, r_sem, to, when=None):
        copy = pltpu.make_async_remote_copy(
            src_ref=src, dst_ref=dst, send_sem=s_sem, recv_sem=r_sem, device_id=to, device_id_type=MESH
        )
        pending.append((copy, when))
        if when is None:
            copy.start()
        else:
            pl.when(when)(copy.start)

    def recv(dst, s_sem, r_sem, to, when=None):
        copy = pltpu.make_async_remote_copy(
            src_ref=dst, dst_ref=dst, send_sem=s_sem, recv_sem=r_sem, device_id=to, device_id_type=MESH
        )
        if when is None:
            copy.wait_recv()
        else:
            pl.when(when)(copy.wait_recv)

    loads = [
        pltpu.make_async_copy(w_hbm.at[i], w_v.at[i], w_sem.at[i]) for i in range(3)
    ]
    loads[1].start()
    loads[2].start()
    wo_load = pltpu.make_async_copy(
        wo_hbm, wo_v.at[pl.ds(pl.multiple_of(t * 768, 768), 768)], w_sem.at[3]
    )

    barrier = pltpu.get_barrier_semaphore()
    for to in (inner, cut, peer, other):
        pl.semaphore_signal(barrier, inc=1, device_id=to, device_id_type=MESH)

    @pl.when(has_up)
    def _():
        pl.semaphore_signal(barrier, inc=1, device_id=upper, device_id_type=MESH)

    @pl.when(has_low)
    def _():
        pl.semaphore_signal(barrier, inc=1, device_id=lower, device_id_type=MESH)

    def normalize(r):
        rows = pl.ds(r * 128, 128)
        x = x_ref[0, rows, :].astype(jnp.float32)
        inv = lax.rsqrt(jnp.mean(x * x, axis=-1, keepdims=True) + EPS)
        nrm[0, rows, :] = (x * inv * (1.0 + mod_ref[1:2, :]) + mod_ref[0:1, :]).astype(jnp.bfloat16)

    def send_normed(r):
        rows = pl.ds(r * 128, 128)
        send(nrm.at[0, rows], nrm.at[1, rows], cut_s.at[r], cut_r.at[r], cut)

    normalize(0)
    pl.semaphore_wait(barrier, 4 + jnp.where(has_up, 1, 0) + jnp.where(has_low, 1, 0))
    send_normed(0)
    normalize(1)
    first_normed = pending.pop()[0]
    send(off_ref, offs, off_sem.at[0], off_sem.at[1], inner)

    slot_of = {A: zlo, B: 1 - zlo, C1: 1 - zlo, D1: zlo, C2: 1 - zlo, D2: zlo}
    group_of = {A: 3, B: 0, C1: 1, D1: 2, C2: 1, D2: 2}
    rows_of = {
        A: pl.ds(0, 256), B: pl.ds(0, 256), C1: pl.ds(0, 128), D1: pl.ds(0, 128),
        C2: pl.ds(128, 128), D2: pl.ds(128, 128),
    }

    def frame(piece, of_core=core):
        return of_core + 2 * slot_of[piece]

    def near_at(side, piece, of_core=core):
        ref = near_a if piece in (A, B) else near_c
        return ref.at[side, frame(piece, of_core), :, rows_of[piece], :]

    def far_at(side, piece, of_core=core):
        ref = far_a if piece in (A, B) else far_c
        return ref.at[side, frame(piece, of_core), :, rows_of[piece], :]

    def q_at(piece):
        return qb.at[group_of[piece], rows_of[piece], :]

    def project(part, nslot, src0, rows, piece):
        st_rows = pl.ds((0, 256, 384)[part], rows)
        own = far_a if part == 0 else far_c
        there = (B, D1, D2)[part]
        for mat in (1, 2, 0):
            if part == 0:
                loads[mat].wait()
                if mat == 1:
                    loads[0].start()
            y = jnp.dot(
                nrm[nslot, src0 : src0 + rows, :], w_v[mat], preferred_element_type=jnp.float32
            )
            thirds = []
            for h in range(6):
                yh = y[:, h * DH : (h + 1) * DH]
                if mat != 2:
                    yh = yh * lax.rsqrt(jnp.mean(yh * yh, axis=-1, keepdims=True) + EPS)
                if mat == 0:
                    yh = yh * hs_ref[h] * (DH ** -0.5)
                thirds.append(yh.astype(jnp.bfloat16))
            for h in range(3):
                lanes = slice(h * DH, (h + 1) * DH)
                mine = jnp.where(zlo == 0, thirds[h], thirds[h + 3])
                theirs = jnp.where(zlo == 0, thirds[h + 3], thirds[h])
                if mat == 0:
                    qb[group_of[piece], rows_of[piece], lanes] = mine
                    st_q[st_rows, lanes] = theirs
                else:
                    own[0, frame(piece), mat - 1, rows_of[piece], lanes] = mine
                    st_kv[mat - 1, st_rows, lanes] = theirs
            if mat == 2:
                send(st_kv.at[:, st_rows], far_at(0, piece), inkv_s.at[part], inkv_r.at[part], inner)
                spread(piece)
            if mat == 0:
                send(st_q.at[st_rows], q_at(there), inq_s.at[part], inq_r.at[part], inner)

    def spread(piece):
        send(far_at(0, piece), near_at(1, piece), y_s.at[UP, piece], y_r.at[UP, piece], upper, has_up)
        send(far_at(0, piece), near_at(0, piece), y_s.at[DOWN, piece], y_r.at[DOWN, piece], lower, has_low)
        send(far_at(0, piece), far_at(0, piece), c0_s.at[piece], c0_r.at[piece], other)

    def from_inner(part, piece):
        recv(far_at(0, piece), inkv_s.at[part], inkv_r.at[part], inner)
        spread(piece)

    def pass_on(piece):
        recv(near_at(1, piece), y_s.at[UP, piece], y_r.at[UP, piece], upper, has_low)
        send(
            near_at(1, piece), far_at(2, piece), f_s.at[UP, piece], f_r.at[UP, piece], upper,
            has_up & has_low & (frame(piece) >= 1),
        )
        send(near_at(1, piece), near_at(1, piece), c1_s.at[UP, piece], c1_r.at[UP, piece], other, has_low)
        recv(near_at(0, piece), y_s.at[DOWN, piece], y_r.at[DOWN, piece], lower, has_up)
        send(
            near_at(0, piece), far_at(1, piece), f_s.at[DOWN, piece], f_r.at[DOWN, piece], lower,
            has_up & has_low & (frame(piece) <= 2),
        )
        send(near_at(0, piece), near_at(0, piece), c1_s.at[DOWN, piece], c1_r.at[DOWN, piece], other, has_up)

    from_up2, from_low2 = col < COLS - 2, col > 1

    def share_far(piece):
        when = from_low2 & (frame(piece) >= 1)
        recv(far_at(2, piece), f_s.at[UP, piece], f_r.at[UP, piece], upper, when)
        send(far_at(2, piece), far_at(2, piece), c2_s.at[UP, piece], c2_r.at[UP, piece], other, when)
        when = from_up2 & (frame(piece) <= 2)
        recv(far_at(1, piece), f_s.at[DOWN, piece], f_r.at[DOWN, piece], lower, when)
        send(far_at(1, piece), far_at(1, piece), c2_s.at[DOWN, piece], c2_r.at[DOWN, piece], other, when)

    j = core + 2 * zlo
    w_rows = 192 // WSUB

    def quarter(half, which, sub):
        return pl.ds(pl.multiple_of(half * 768 + which * 192 + sub * w_rows, 16), w_rows)

    other_j, inner_j = j + 1 - 2 * core, j + 2 - 4 * zlo
    diag_j = 3 - j

    def wo_cut(sub):
        src = pl.ds(pl.multiple_of(inner_j * 192 + sub * w_rows, 16), w_rows)
        send(wo_hbm.at[src], wo_v.at[quarter(t, inner_j, sub)], wc_s.at[sub], wc_r.at[sub], cut)

    def wo_share(sub):
        mine = wo_v.at[quarter(1 - t, j, sub)]
        recv(mine, wc_s.at[sub], wc_r.at[sub], cut)
        send(mine, mine, wi_s.at[sub], wi_r.at[sub], inner)
        send(mine, mine, wk_s.at[sub], wk_r.at[sub], other)

    def wo_second(sub):
        theirs = wo_v.at[quarter(1 - t, inner_j, sub)]
        recv(theirs, wi_s.at[sub], wi_r.at[sub], inner)
        send(theirs, theirs, wj_s.at[sub], wj_r.at[sub], other)

    def wo_last(sub):
        recv(wo_v.at[quarter(1 - t, other_j, sub)], wk_s.at[sub], wk_r.at[sub], other)
        recv(wo_v.at[quarter(1 - t, diag_j, sub)], wj_s.at[sub], wj_r.at[sub], other)

    project(0, 0, 0, 256, A)
    first_normed.wait_send()
    send_normed(1)
    wo_load.start()

    @pl.when(col == COLS - 1)
    def _():
        near_a[0] = jnp.zeros_like(near_a[0])
        near_c[0] = jnp.zeros_like(near_c[0])

    @pl.when(col == 0)
    def _():
        near_a[1] = jnp.zeros_like(near_a[1])
        near_c[1] = jnp.zeros_like(near_c[1])

    @pl.when(col >= COLS - 2)
    def _():
        far_a[1] = jnp.zeros_like(far_a[1])
        far_c[1] = jnp.zeros_like(far_c[1])

    @pl.when(col <= 1)
    def _():
        far_a[2] = jnp.zeros_like(far_a[2])
        far_c[2] = jnp.zeros_like(far_c[2])

    def place_of(unit):
        group, h = unit // 3, lax.rem(unit, 3)
        slot = jnp.where(group < 2, 1 - zlo, zlo)
        return group, slot, pl.ds(pl.multiple_of(h * DH, DH), DH)

    def near_blocks(slot, ref, own):
        mine = core + 2 * slot
        o = jnp.where(slot == zlo, off_ref[0], offs[0])
        blocks = [(own, (0, mine), None)]
        for i in range(4):
            below = 4 + i - mine > WIN - 1 - o
            side = jnp.where(below, 1, 0)
            blocks.append((ref, (side, i), jnp.where(below, has_low, has_up)))
        return blocks

    def far_blocks(slot, ref):
        mine = core + 2 * slot
        o = jnp.where(slot == zlo, off_ref[0], offs[0])
        blocks = []
        for n in range(3):
            r = n + jnp.where(n >= mine, 1, 0)
            less = r < mine
            inside = jnp.where(less, mine - r <= o, r - mine <= WIN - 1 - o)
            side = jnp.where(inside, 0, jnp.where(less, 1, 2))
            blocks.append((ref, (side, r), inside | jnp.where(less, from_up2, from_low2)))
        return blocks

    def stage_blocks(stage, slot):
        if stage == 0:
            return near_blocks(slot, near_a, far_a) + far_blocks(slot, far_a)
        if stage == 1:
            return near_blocks(slot, near_c, far_c)
        return far_blocks(slot, far_c)

    COUNT = (8, 5, 3)

    def score(stage, unit, b, buf, top):
        group, slot, lanes = place_of(unit)
        ref, lead, valid = stage_blocks(stage, slot)[b]
        s = lax.dot_general(
            qb[group, :, lanes], ref[(*lead, 0, slice(None), lanes)],
            (((1,), (1,)), ((), ())), preferred_element_type=jnp.float32,
        )
        buf[:, b * HALF : (b + 1) * HALF] = s
        high = jnp.maximum(s[:, :DH], s[:, DH:])
        if valid is not None:
            high = jnp.where(valid, high, LOW)
        return high if top is None else jnp.maximum(top, high)

    def peak(stage, unit, top):
        high = jnp.broadcast_to(jnp.max(top, axis=1, keepdims=True), (HALF, DH))
        if stage > 0:
            before = m_s[unit]
            high = jnp.maximum(high, before)
            scale = jnp.exp(before - high)
            acc_s[unit] = acc_s[unit] * scale
            l_s[unit] = l_s[unit] * scale
        m_s[unit] = high

    def weigh(stage, unit, b, buf, high, total, weighted):
        _, slot, lanes = place_of(unit)
        ref, lead, valid = stage_blocks(stage, slot)[b]
        base = high if valid is None else jnp.where(valid, high, HIGH)
        p = [jnp.exp(buf[:, b * HALF + c * DH : b * HALF + (c + 1) * DH] - base) for c in range(2)]
        part = p[0] + p[1]
        rounded = jnp.concatenate([c.astype(jnp.bfloat16) for c in p], axis=1)
        o = jnp.dot(rounded, ref[(*lead, 1, slice(None), lanes)], preferred_element_type=jnp.float32)
        return (part if total is None else total + part), (o if weighted is None else weighted + o)

    def finish(stage, unit, total, weighted):
        if stage > 0:
            total = total + l_s[unit]
            weighted = weighted + acc_s[unit]
        if stage < 2:
            l_s[unit] = total
            acc_s[unit] = weighted
        else:
            group, _, lanes = place_of(unit)
            ob[group, :, lanes] = (weighted / jnp.sum(total, axis=1, keepdims=True)).astype(jnp.bfloat16)

    def start_unit(stage, unit, buf):
        top = None
        for b in range(COUNT[stage]):
            top = score(stage, unit, b, buf, top)
        peak(stage, unit, top)

    def step(stage, unit, buf, following, other_buf):
        high = m_s[unit]
        top = total = weighted = None
        for b in range(COUNT[stage]):
            if following is not None:
                top = score(stage, following, b, other_buf, top)
            total, weighted = weigh(stage, unit, b, buf, high, total, weighted)
        finish(stage, unit, total, weighted)
        if following is not None:
            peak(stage, following, top)

    def units(stage, low, high):
        start_unit(stage, low, even)

        def two(i, carry):
            unit = low + 2 * i
            step(stage, unit, even, unit + 1, odd)
            step(stage, unit + 1, odd, jnp.minimum(unit + 2, high - 1), even)
            return carry

        lax.fori_loop(0, (high - low) // 2, two, 0)

    def near_from_core(*pieces):
        for piece in pieces:
            recv(near_at(1, piece, 1 - core), c1_s.at[UP, piece], c1_r.at[UP, piece], other, has_low)
            recv(near_at(0, piece, 1 - core), c1_s.at[DOWN, piece], c1_r.at[DOWN, piece], other, has_up)

    def own_from_core(*pieces):
        for piece in pieces:
            recv(far_at(0, piece, 1 - core), c0_s.at[piece], c0_r.at[piece], other)

    def far_from_core(*pieces):
        for piece in pieces:
            recv(
                far_at(2, piece, 1 - core), c2_s.at[UP, piece], c2_r.at[UP, piece], other,
                from_low2 & (frame(piece, 1 - core) >= 1),
            )
            recv(
                far_at(1, piece, 1 - core), c2_s.at[DOWN, piece], c2_r.at[DOWN, piece], other,
                from_up2 & (frame(piece, 1 - core) <= 2),
            )

    from_inner(0, B)
    pass_on(A)
    recv(nrm.at[1, pl.ds(0, 128)], cut_s.at[0], cut_r.at[0], cut)
    project(1, 1, 0, 128, C1)
    pass_on(B)
    from_inner(1, D1)
    recv(nrm.at[1, pl.ds(128, 128)], cut_s.at[1], cut_r.at[1], cut)
    for sub in range(WSUB):
        wo_cut(sub)
    project(2, 1, 128, 128, C2)
    pass_on(C1)
    pass_on(D1)
    from_inner(2, D2)
    share_far(A)
    share_far(B)
    wo_share(0)
    recv(offs, off_sem.at[0], off_sem.at[1], inner)
    for part, piece in ((0, B), (1, D1), (2, D2)):
        recv(q_at(piece), inq_s.at[part], inq_r.at[part], inner)
    near_from_core(A, B)
    own_from_core(A, B)
    far_from_core(A, B)
    units(0, 0, 6)
    pass_on(C2)
    wo_share(1)
    wo_second(0)
    units(0, 6, 12)
    pass_on(D2)
    share_far(C1)
    share_far(D1)
    wo_share(2)
    wo_second(1)
    near_from_core(C1, D1, C2, D2)
    own_from_core(C1, D1, C2, D2)
    units(1, 0, 6)
    wo_share(3)
    wo_second(2)
    units(1, 6, 12)
    share_far(C2)
    share_far(D2)
    wo_second(3)
    far_from_core(C1, D1, C2, D2)

    triple = 2 * t + zlo
    goes_to = (inner, cut, peer)
    start_unit(2, 0, even)
    for unit in range(12):
        bufs = (even, odd) if unit % 2 == 0 else (odd, even)
        step(2, unit, bufs[0], unit + 1 if unit < 11 else None, bufs[1])
        if unit % 3 == 2 and unit < 9:
            n = unit // 3
            send(ob.at[n], att.at[triple], o_s.at[n], o_r.at[n], goes_to[n])
    att[triple] = ob[3]

    def joined(half):
        return jnp.concatenate([att[2 * half], att[2 * half + 1]], axis=1)

    def out_rows(half):
        return pl.ds(pl.multiple_of(half * 768, 768), 768)

    wo_load.wait()
    recv(att.at[2 * t + 1 - zlo], o_s.at[0], o_r.at[0], inner)
    left = joined(t)
    for n in range(D // 512):
        buf, at = (even, n * 512) if n < 4 else (odd, (n - 4) * 512)
        buf[:, at : at + 512] = jnp.dot(
            left, wo_v[out_rows(t), n * 512 : (n + 1) * 512], preferred_element_type=jnp.float32
        )
    for sub in range(WSUB):
        wo_last(sub)
    recv(att.at[2 * (1 - t) + 1 - zlo], o_s.at[1], o_r.at[1], cut)
    recv(att.at[2 * (1 - t) + zlo], o_s.at[2], o_r.at[2], peer)
    right = joined(1 - t)
    for n in range(D // 512):
        buf, at = (even, n * 512) if n < 4 else (odd, (n - 4) * 512)
        lanes = slice(n * 512, (n + 1) * 512)
        branch = buf[:, at : at + 512] + jnp.dot(
            right, wo_v[out_rows(1 - t), lanes], preferred_element_type=jnp.float32
        )
        x = x_ref[0, :, lanes].astype(jnp.float32)
        out_ref[0, :, lanes] = (x + mod_ref[2:3, lanes] * branch).astype(jnp.bfloat16)
    for copy, when in pending:
        if when is None:
            copy.wait_send()
        else:
            pl.when(when)(copy.wait_send)


def shards(latents, levels, offsets, level_table, w_qkv, w_out, head_scale):
    table = jnp.transpose(level_table, (1, 0, 2))
    modulation = lax.dynamic_index_in_dim(table, levels[0], 1, keepdims=False)
    weights = jnp.transpose(w_qkv, (1, 0, 2))
    bf, f32 = jnp.bfloat16, jnp.float32
    dma = pltpu.SemaphoreType.DMA
    vmem = pl.BlockSpec(memory_space=pltpu.VMEM)
    smem = pl.BlockSpec(memory_space=pltpu.SMEM)
    hbm = pl.BlockSpec(memory_space=pl.ANY)
    pair = lambda *n: [dma(n), dma(n)]
    return pl.pallas_call(
        body,
        out_shape=jax.ShapeDtypeStruct((1, HALF, D), bf),
        in_specs=[vmem, vmem, hbm, hbm, smem, smem],
        out_specs=vmem,
        scratch_shapes=[
            pltpu.VMEM((2, 4, 2, HALF, TRI), bf),
            pltpu.VMEM((2, 4, 2, HALF, TRI), bf),
            pltpu.VMEM((3, 4, 2, HALF, TRI), bf),
            pltpu.VMEM((3, 4, 2, HALF, TRI), bf),
            pltpu.VMEM((4, HALF, TRI), bf),
            pltpu.VMEM((3, D, 768), bf),
            pltpu.VMEM((1536, D), bf),
            pltpu.VMEM((2, HALF, D), bf),
            pltpu.VMEM((2, TOK, TRI), bf),
            pltpu.VMEM((TOK, TRI), bf),
            pltpu.VMEM((HALF, 8 * HALF), f32),
            pltpu.VMEM((HALF, 8 * HALF), f32),
            pltpu.VMEM((12, HALF, DH), f32),
            pltpu.VMEM((12, HALF, DH), f32),
            pltpu.VMEM((12, HALF, DH), f32),
            pltpu.VMEM((4, HALF, TRI), bf),
            pltpu.VMEM((4, HALF, TRI), bf),
            pltpu.SMEM((1,), jnp.int32),
            dma((4,)), dma((2,)),
            *pair(2), *pair(3), *pair(3), *pair(2, 6), *pair(2, 6),
            *pair(6), *pair(2, 6), *pair(2, 6),
            *pair(WSUB), *pair(WSUB), *pair(WSUB), *pair(WSUB), *pair(3),
        ],
        compiler_params=pltpu.CompilerParams(
            collective_id=0, has_side_effects=True, vmem_limit_bytes=62 * 2**20
        ),
        cost_estimate=pl.CostEstimate(flops=17 * 10**9, bytes_accessed=25 * 10**6, transcendentals=13 * 10**6),
        name="frame_attention",
    )(latents, modulation, weights, w_out, offsets, head_scale)


def solution(mesh):
    placed = (
        P("queue", "tok", None),
        P("queue"),
        P("queue"),
        P(),
        P(None, None, "tok"),
        P("tok", None),
        P("tok"),
    )
    return jax.shard_map(
        shards, mesh=mesh, in_specs=placed, out_specs=P("queue", "tok", None), check_vma=False
    )
```

```python
import functools

import jax
import jax.numpy as jnp
from jax import lax
from jax.experimental import pallas as pl
from jax.experimental.pallas import tpu as pltpu
from jax.sharding import PartitionSpec as P

D = 3072
DH = 128
WIN = 8
TOK = 512
HALF = 256
TRI = 384
COLS = 16
EPS = 1e-6
LOW = -1e30
HIGH = 1e30
WSUB = 4
MESH = pl.DeviceIdType.MESH
UP, DOWN = 0, 1
A, B, C1, D1, C2, D2 = range(6)


def body(
    x_ref, mod_ref, w_hbm, wo_hbm, off_ref, hs_ref,
    out_ref,
    near_a, near_c, far_a, far_c, qb, w_v, wo_v, nrm, st_kv, st_q, even, odd, acc_s, m_s, l_s, att, ob, offs,
    w_sem, off_sem, cut_s, cut_r, inkv_s, inkv_r, inq_s, inq_r, y_s, y_r, f_s, f_r,
    c0_s, c0_r, c1_s, c1_r, c2_s, c2_r, wc_s, wc_r, wi_s, wi_r, wk_s, wk_r, wj_s, wj_r, o_s, o_r,
):
    q = lax.axis_index("queue")
    t = lax.axis_index("tok")
    core = lax.rem(q, 2)
    zlo = lax.rem(q // 2, 2)
    col = q // 4
    inner_q = q + 2 - 4 * zlo
    inner = (inner_q, t)
    cut = (inner_q, 1 - t)
    peer = (q, 1 - t)
    other = (q + 1 - 2 * core, t)
    upper = (q + 4, t)
    lower = (q - 4, t)
    has_up, has_low = col < COLS - 1, col > 0
    pending = []

    def send(src, dst, s_sem, r_sem, to, when=None):
        copy = pltpu.make_async_remote_copy(
            src_ref=src, dst_ref=dst, send_sem=s_sem, recv_sem=r_sem, device_id=to, device_id_type=MESH
        )
        pending.append((copy, when))
        if when is None:
            copy.start()
        else:
            pl.when(when)(copy.start)

    def recv(dst, s_sem, r_sem, to, when=None):
        copy = pltpu.make_async_remote_copy(
            src_ref=dst, dst_ref=dst, send_sem=s_sem, recv_sem=r_sem, device_id=to, device_id_type=MESH
        )
        if when is None:
            copy.wait_recv()
        else:
            pl.when(when)(copy.wait_recv)

    loads = [
        pltpu.make_async_copy(w_hbm.at[i], w_v.at[i], w_sem.at[i]) for i in range(3)
    ]
    loads[1].start()
    loads[2].start()
    wo_load = pltpu.make_async_copy(
        wo_hbm, wo_v.at[pl.ds(pl.multiple_of(t * 768, 768), 768)], w_sem.at[3]
    )

    barrier = pltpu.get_barrier_semaphore()
    for to in (inner, cut, peer, other):
        pl.semaphore_signal(barrier, inc=1, device_id=to, device_id_type=MESH)

    @pl.when(has_up)
    def _():
        pl.semaphore_signal(barrier, inc=1, device_id=upper, device_id_type=MESH)

    @pl.when(has_low)
    def _():
        pl.semaphore_signal(barrier, inc=1, device_id=lower, device_id_type=MESH)

    def normalize(r):
        rows = pl.ds(r * 128, 128)
        x = x_ref[0, rows, :].astype(jnp.float32)
        inv = lax.rsqrt(jnp.mean(x * x, axis=-1, keepdims=True) + EPS)
        nrm[0, rows, :] = (x * inv * (1.0 + mod_ref[1:2, :]) + mod_ref[0:1, :]).astype(jnp.bfloat16)

    def send_normed(r):
        rows = pl.ds(r * 128, 128)
        send(nrm.at[0, rows], nrm.at[1, rows], cut_s.at[r], cut_r.at[r], cut)

    normalize(0)
    pl.semaphore_wait(barrier, 4 + jnp.where(has_up, 1, 0) + jnp.where(has_low, 1, 0))
    send_normed(0)
    normalize(1)
    first_normed = pending.pop()[0]
    send(off_ref, offs, off_sem.at[0], off_sem.at[1], inner)

    slot_of = {A: zlo, B: 1 - zlo, C1: 1 - zlo, D1: zlo, C2: 1 - zlo, D2: zlo}
    group_of = {A: 0, B: 1, C1: 2, D1: 3, C2: 2, D2: 3}
    rows_of = {
        A: pl.ds(0, 256), B: pl.ds(0, 256), C1: pl.ds(0, 128), D1: pl.ds(0, 128),
        C2: pl.ds(128, 128), D2: pl.ds(128, 128),
    }

    def frame(piece, of_core=core):
        return of_core + 2 * slot_of[piece]

    def near_at(side, piece, of_core=core):
        ref = near_a if piece in (A, B) else near_c
        return ref.at[side, frame(piece, of_core), :, rows_of[piece], :]

    def far_at(side, piece, of_core=core):
        ref = far_a if piece in (A, B) else far_c
        return ref.at[side, frame(piece, of_core), :, rows_of[piece], :]

    def q_at(piece):
        return qb.at[group_of[piece], rows_of[piece], :]

    def project(part, nslot, src0, rows, piece):
        st_rows = pl.ds((0, 256, 384)[part], rows)
        own = far_a if part == 0 else far_c
        there = (B, D1, D2)[part]
        for mat in (1, 2, 0):
            if part == 0:
                loads[mat].wait()
                if mat == 1:
                    loads[0].start()
            y = jnp.dot(
                nrm[nslot, src0 : src0 + rows, :], w_v[mat], preferred_element_type=jnp.float32
            )
            thirds = []
            for h in range(6):
                yh = y[:, h * DH : (h + 1) * DH]
                if mat != 2:
                    yh = yh * lax.rsqrt(jnp.mean(yh * yh, axis=-1, keepdims=True) + EPS)
                if mat == 0:
                    yh = yh * hs_ref[h] * (DH ** -0.5)
                thirds.append(yh.astype(jnp.bfloat16))
            for h in range(3):
                lanes = slice(h * DH, (h + 1) * DH)
                mine = jnp.where(zlo == 0, thirds[h], thirds[h + 3])
                theirs = jnp.where(zlo == 0, thirds[h + 3], thirds[h])
                if mat == 0:
                    qb[group_of[piece], rows_of[piece], lanes] = mine
                    st_q[st_rows, lanes] = theirs
                else:
                    own[0, frame(piece), mat - 1, rows_of[piece], lanes] = mine
                    st_kv[mat - 1, st_rows, lanes] = theirs
            if mat == 2:
                send(st_kv.at[:, st_rows], far_at(0, piece), inkv_s.at[part], inkv_r.at[part], inner)
                spread(piece)
            if mat == 0:
                send(st_q.at[st_rows], q_at(there), inq_s.at[part], inq_r.at[part], inner)

    def spread(piece):
        send(far_at(0, piece), near_at(1, piece), y_s.at[UP, piece], y_r.at[UP, piece], upper, has_up)
        send(far_at(0, piece), near_at(0, piece), y_s.at[DOWN, piece], y_r.at[DOWN, piece], lower, has_low)
        send(far_at(0, piece), far_at(0, piece), c0_s.at[piece], c0_r.at[piece], other)

    def from_inner(part, piece):
        recv(far_at(0, piece), inkv_s.at[part], inkv_r.at[part], inner)
        spread(piece)

    def pass_on(piece):
        recv(near_at(1, piece), y_s.at[UP, piece], y_r.at[UP, piece], upper, has_low)
        send(
            near_at(1, piece), far_at(2, piece), f_s.at[UP, piece], f_r.at[UP, piece], upper,
            has_up & has_low & (frame(piece) >= 1),
        )
        send(near_at(1, piece), near_at(1, piece), c1_s.at[UP, piece], c1_r.at[UP, piece], other, has_low)
        recv(near_at(0, piece), y_s.at[DOWN, piece], y_r.at[DOWN, piece], lower, has_up)
        send(
            near_at(0, piece), far_at(1, piece), f_s.at[DOWN, piece], f_r.at[DOWN, piece], lower,
            has_up & has_low & (frame(piece) <= 2),
        )
        send(near_at(0, piece), near_at(0, piece), c1_s.at[DOWN, piece], c1_r.at[DOWN, piece], other, has_up)

    from_up2, from_low2 = col < COLS - 2, col > 1

    def share_far(piece):
        when = from_low2 & (frame(piece) >= 1)
        recv(far_at(2, piece), f_s.at[UP, piece], f_r.at[UP, piece], upper, when)
        send(far_at(2, piece), far_at(2, piece), c2_s.at[UP, piece], c2_r.at[UP, piece], other, when)
        when = from_up2 & (frame(piece) <= 2)
        recv(far_at(1, piece), f_s.at[DOWN, piece], f_r.at[DOWN, piece], lower, when)
        send(far_at(1, piece), far_at(1, piece), c2_s.at[DOWN, piece], c2_r.at[DOWN, piece], other, when)

    j = core + 2 * zlo
    w_rows = 192 // WSUB

    def quarter(half, which, sub):
        return pl.ds(pl.multiple_of(half * 768 + which * 192 + sub * w_rows, 16), w_rows)

    other_j, inner_j = j + 1 - 2 * core, j + 2 - 4 * zlo
    diag_j = 3 - j

    def wo_cut(sub):
        src = pl.ds(pl.multiple_of(inner_j * 192 + sub * w_rows, 16), w_rows)
        send(wo_hbm.at[src], wo_v.at[quarter(t, inner_j, sub)], wc_s.at[sub], wc_r.at[sub], cut)

    def wo_share(sub):
        mine = wo_v.at[quarter(1 - t, j, sub)]
        recv(mine, wc_s.at[sub], wc_r.at[sub], cut)
        send(mine, mine, wi_s.at[sub], wi_r.at[sub], inner)
        send(mine, mine, wk_s.at[sub], wk_r.at[sub], other)

    def wo_second(sub):
        theirs = wo_v.at[quarter(1 - t, inner_j, sub)]
        recv(theirs, wi_s.at[sub], wi_r.at[sub], inner)
        send(theirs, theirs, wj_s.at[sub], wj_r.at[sub], other)

    def wo_last(sub):
        recv(wo_v.at[quarter(1 - t, other_j, sub)], wk_s.at[sub], wk_r.at[sub], other)
        recv(wo_v.at[quarter(1 - t, diag_j, sub)], wj_s.at[sub], wj_r.at[sub], other)

    project(0, 0, 0, 256, A)
    first_normed.wait_send()
    send_normed(1)
    wo_load.start()

    @pl.when(col == COLS - 1)
    def _():
        near_a[0] = jnp.zeros_like(near_a[0])
        near_c[0] = jnp.zeros_like(near_c[0])

    @pl.when(col == 0)
    def _():
        near_a[1] = jnp.zeros_like(near_a[1])
        near_c[1] = jnp.zeros_like(near_c[1])

    @pl.when(col >= COLS - 2)
    def _():
        far_a[1] = jnp.zeros_like(far_a[1])
        far_c[1] = jnp.zeros_like(far_c[1])

    @pl.when(col <= 1)
    def _():
        far_a[2] = jnp.zeros_like(far_a[2])
        far_c[2] = jnp.zeros_like(far_c[2])

    def place_of(unit):
        group, h = unit // 3, lax.rem(unit, 3)
        slot = jnp.where((group == 0) | (group == 3), zlo, 1 - zlo)
        return group, slot, pl.ds(pl.multiple_of(h * DH, DH), DH)

    def near_blocks(slot, ref, own):
        mine = core + 2 * slot
        o = jnp.where(slot == zlo, off_ref[0], offs[0])
        blocks = [(own, (0, mine), None)]
        for i in range(4):
            below = 4 + i - mine > WIN - 1 - o
            side = jnp.where(below, 1, 0)
            blocks.append((ref, (side, i), jnp.where(below, has_low, has_up)))
        return blocks

    def far_blocks(slot, ref):
        mine = core + 2 * slot
        o = jnp.where(slot == zlo, off_ref[0], offs[0])
        blocks = []
        for n in range(3):
            r = n + jnp.where(n >= mine, 1, 0)
            less = r < mine
            inside = jnp.where(less, mine - r <= o, r - mine <= WIN - 1 - o)
            side = jnp.where(inside, 0, jnp.where(less, 1, 2))
            blocks.append((ref, (side, r), inside | jnp.where(less, from_up2, from_low2)))
        return blocks

    def stage_blocks(stage, slot):
        if stage == 0:
            return near_blocks(slot, near_a, far_a)
        if stage == 1:
            return far_blocks(slot, far_a)
        if stage == 2:
            return near_blocks(slot, near_c, far_c)
        return far_blocks(slot, far_c)

    COUNT = (5, 3, 5, 3)

    def score(stage, unit, b, buf, top):
        group, slot, lanes = place_of(unit)
        ref, lead, valid = stage_blocks(stage, slot)[b]
        s = lax.dot_general(
            qb[group, :, lanes], ref[(*lead, 0, slice(None), lanes)],
            (((1,), (1,)), ((), ())), preferred_element_type=jnp.float32,
        )
        buf[:, b * HALF : (b + 1) * HALF] = s
        high = jnp.maximum(s[:, :DH], s[:, DH:])
        if valid is not None:
            high = jnp.where(valid, high, LOW)
        return high if top is None else jnp.maximum(top, high)

    def peak(stage, unit, top):
        high = jnp.broadcast_to(jnp.max(top, axis=1, keepdims=True), (HALF, DH))
        if stage > 0:
            before = m_s[unit]
            high = jnp.maximum(high, before)
            scale = jnp.exp(before - high)
            acc_s[unit] = acc_s[unit] * scale
            l_s[unit] = l_s[unit] * scale
        m_s[unit] = high

    def weigh(stage, unit, b, buf, high, total, weighted):
        _, slot, lanes = place_of(unit)
        ref, lead, valid = stage_blocks(stage, slot)[b]
        base = high if valid is None else jnp.where(valid, high, HIGH)
        p = [jnp.exp(buf[:, b * HALF + c * DH : b * HALF + (c + 1) * DH] - base) for c in range(2)]
        part = p[0] + p[1]
        rounded = jnp.concatenate([c.astype(jnp.bfloat16) for c in p], axis=1)
        o = jnp.dot(rounded, ref[(*lead, 1, slice(None), lanes)], preferred_element_type=jnp.float32)
        return (part if total is None else total + part), (o if weighted is None else weighted + o)

    def finish(stage, unit, total, weighted):
        if stage > 0:
            total = total + l_s[unit]
            weighted = weighted + acc_s[unit]
        if stage < 3:
            l_s[unit] = total
            acc_s[unit] = weighted
        else:
            group, _, lanes = place_of(unit)
            ob[group, :, lanes] = (weighted / jnp.sum(total, axis=1, keepdims=True)).astype(jnp.bfloat16)

    def start_unit(stage, unit, buf):
        top = None
        for b in range(COUNT[stage]):
            top = score(stage, unit, b, buf, top)
        peak(stage, unit, top)

    def step(stage, unit, buf, following, other_buf):
        high = m_s[unit]
        top = total = weighted = None
        for b in range(COUNT[stage]):
            if following is not None:
                top = score(stage, following, b, other_buf, top)
            total, weighted = weigh(stage, unit, b, buf, high, total, weighted)
        finish(stage, unit, total, weighted)
        if following is not None:
            peak(stage, following, top)

    def units(stage, low, high):
        start_unit(stage, low, even)

        def two(i, carry):
            unit = low + 2 * i
            step(stage, unit, even, unit + 1, odd)
            step(stage, unit + 1, odd, jnp.minimum(unit + 2, high - 1), even)
            return carry

        lax.fori_loop(0, (high - low) // 2, two, 0)

    def near_from_core(*pieces):
        for piece in pieces:
            recv(near_at(1, piece, 1 - core), c1_s.at[UP, piece], c1_r.at[UP, piece], other, has_low)
            recv(near_at(0, piece, 1 - core), c1_s.at[DOWN, piece], c1_r.at[DOWN, piece], other, has_up)

    def own_from_core(*pieces):
        for piece in pieces:
            recv(far_at(0, piece, 1 - core), c0_s.at[piece], c0_r.at[piece], other)

    def far_from_core(*pieces):
        for piece in pieces:
            recv(
                far_at(2, piece, 1 - core), c2_s.at[UP, piece], c2_r.at[UP, piece], other,
                from_low2 & (frame(piece, 1 - core) >= 1),
            )
            recv(
                far_at(1, piece, 1 - core), c2_s.at[DOWN, piece], c2_r.at[DOWN, piece], other,
                from_up2 & (frame(piece, 1 - core) <= 2),
            )

    from_inner(0, B)
    pass_on(A)
    recv(nrm.at[1, pl.ds(0, 128)], cut_s.at[0], cut_r.at[0], cut)
    project(1, 1, 0, 128, C1)
    pass_on(B)
    from_inner(1, D1)
    recv(offs, off_sem.at[0], off_sem.at[1], inner)
    recv(q_at(B), inq_s.at[0], inq_r.at[0], inner)
    near_from_core(A, B)
    own_from_core(A, B)
    units(0, 0, 6)
    recv(nrm.at[1, pl.ds(128, 128)], cut_s.at[1], cut_r.at[1], cut)
    wo_cut(0)
    wo_cut(1)
    project(2, 1, 128, 128, C2)
    from_inner(2, D2)
    wo_cut(2)
    wo_cut(3)
    recv(q_at(D1), inq_s.at[1], inq_r.at[1], inner)
    recv(q_at(D2), inq_s.at[2], inq_r.at[2], inner)
    units(0, 6, 12)
    pass_on(C1)
    pass_on(D1)
    pass_on(C2)
    wo_share(0)
    wo_share(1)
    share_far(A)
    share_far(B)
    far_from_core(A, B)
    units(1, 0, 6)
    pass_on(D2)
    units(1, 6, 12)
    wo_share(2)
    wo_share(3)
    share_far(C1)
    share_far(D1)
    near_from_core(C1, D1, C2, D2)
    own_from_core(C1, D1, C2, D2)
    units(2, 0, 6)
    wo_second(0)
    wo_second(1)
    units(2, 6, 12)
    share_far(C2)
    share_far(D2)
    far_from_core(C1, D1, C2, D2)

    triple = 2 * t + zlo
    goes_to = (None, inner, cut, peer)
    order = (3, 4, 5, 6, 7, 8, 9, 10, 11, 0, 1, 2)
    start_unit(3, order[0], even)
    for n, unit in enumerate(order):
        bufs = (even, odd) if n % 2 == 0 else (odd, even)
        step(3, unit, bufs[0], order[n + 1] if n < 11 else None, bufs[1])
        group = unit // 3
        if unit % 3 == 2 and group > 0:
            send(ob.at[group], att.at[triple], o_s.at[group - 1], o_r.at[group - 1], goes_to[group])
    att[triple] = ob[0]
    wo_second(2)
    wo_second(3)

    def joined(half):
        return jnp.concatenate([att[2 * half], att[2 * half + 1]], axis=1)

    def out_rows(half):
        return pl.ds(pl.multiple_of(half * 768, 768), 768)

    wo_load.wait()
    recv(att.at[2 * t + 1 - zlo], o_s.at[0], o_r.at[0], inner)
    left = joined(t)
    for n in range(D // 512):
        buf, at = (even, n * 512) if n < 3 else (odd, (n - 3) * 512)
        buf[:, at : at + 512] = jnp.dot(
            left, wo_v[out_rows(t), n * 512 : (n + 1) * 512], preferred_element_type=jnp.float32
        )
    for sub in range(WSUB):
        wo_last(sub)
    recv(att.at[2 * (1 - t) + 1 - zlo], o_s.at[1], o_r.at[1], cut)
    recv(att.at[2 * (1 - t) + zlo], o_s.at[2], o_r.at[2], peer)
    right = joined(1 - t)
    for n in range(D // 512):
        buf, at = (even, n * 512) if n < 3 else (odd, (n - 3) * 512)
        lanes = slice(n * 512, (n + 1) * 512)
        branch = buf[:, at : at + 512] + jnp.dot(
            right, wo_v[out_rows(1 - t), lanes], preferred_element_type=jnp.float32
        )
        x = x_ref[0, :, lanes].astype(jnp.float32)
        out_ref[0, :, lanes] = (x + mod_ref[2:3, lanes] * branch).astype(jnp.bfloat16)
    for copy, when in pending:
        if when is None:
            copy.wait_send()
        else:
            pl.when(when)(copy.wait_send)


def shards(latents, levels, offsets, level_table, w_qkv, w_out, head_scale):
    table = jnp.transpose(level_table, (1, 0, 2))
    modulation = lax.dynamic_index_in_dim(table, levels[0], 1, keepdims=False)
    weights = jnp.transpose(w_qkv, (1, 0, 2))
    bf, f32 = jnp.bfloat16, jnp.float32
    dma = pltpu.SemaphoreType.DMA
    vmem = pl.BlockSpec(memory_space=pltpu.VMEM)
    smem = pl.BlockSpec(memory_space=pltpu.SMEM)
    hbm = pl.BlockSpec(memory_space=pl.ANY)
    pair = lambda *n: [dma(n), dma(n)]
    return pl.pallas_call(
        body,
        out_shape=jax.ShapeDtypeStruct((1, HALF, D), bf),
        in_specs=[vmem, vmem, hbm, hbm, smem, smem],
        out_specs=vmem,
        scratch_shapes=[
            pltpu.VMEM((2, 4, 2, HALF, TRI), bf),
            pltpu.VMEM((2, 4, 2, HALF, TRI), bf),
            pltpu.VMEM((3, 4, 2, HALF, TRI), bf),
            pltpu.VMEM((3, 4, 2, HALF, TRI), bf),
            pltpu.VMEM((4, HALF, TRI), bf),
            pltpu.VMEM((3, D, 768), bf),
            pltpu.VMEM((1536, D), bf),
            pltpu.VMEM((2, HALF, D), bf),
            pltpu.VMEM((2, TOK, TRI), bf),
            pltpu.VMEM((TOK, TRI), bf),
            pltpu.VMEM((HALF, D // 2), f32),
            pltpu.VMEM((HALF, D // 2), f32),
            pltpu.VMEM((12, HALF, DH), f32),
            pltpu.VMEM((12, HALF, DH), f32),
            pltpu.VMEM((12, HALF, DH), f32),
            pltpu.VMEM((4, HALF, TRI), bf),
            pltpu.VMEM((4, HALF, TRI), bf),
            pltpu.SMEM((1,), jnp.int32),
            dma((4,)), dma((2,)),
            *pair(2), *pair(3), *pair(3), *pair(2, 6), *pair(2, 6),
            *pair(6), *pair(2, 6), *pair(2, 6),
            *pair(WSUB), *pair(WSUB), *pair(WSUB), *pair(WSUB), *pair(3),
        ],
        compiler_params=pltpu.CompilerParams(
            collective_id=0, has_side_effects=True, vmem_limit_bytes=62 * 2**20
        ),
        cost_estimate=pl.CostEstimate(flops=17 * 10**9, bytes_accessed=25 * 10**6, transcendentals=13 * 10**6),
        name="frame_attention",
    )(latents, modulation, weights, w_out, offsets, head_scale)


def solution(mesh):
    placed = (
        P("queue", "tok", None),
        P("queue"),
        P("queue"),
        P(),
        P(None, None, "tok"),
        P("tok", None),
        P("tok"),
    )
    return jax.shard_map(
        shards, mesh=mesh, in_specs=placed, out_specs=P("queue", "tok", None), check_vma=False
    )
```

```python
import functools

import jax
import jax.numpy as jnp
from jax import lax
from jax.experimental import pallas as pl
from jax.experimental.pallas import tpu as pltpu
from jax.sharding import PartitionSpec as P

D = 3072
DH = 128
WIN = 8
TOK = 512
HALF = 256
TRI = 384
COLS = 16
EPS = 1e-6
LOW = -1e30
HIGH = 1e30
WSUB = 4
MESH = pl.DeviceIdType.MESH
UP, DOWN = 0, 1
A, B, C1, D1, C2, D2 = range(6)


def body(
    x_ref, mod_ref, w_hbm, wo_hbm, off_ref, hs_ref,
    out_ref,
    near_a, near_c, far_a, far_c, qb, w_v, wo_v, nrm, st_kv, st_q, even, odd, acc_s, m_s, l_s, att, ob, offs,
    w_sem, off_sem, cut_s, cut_r, inkv_s, inkv_r, inq_s, inq_r, y_s, y_r, f_s, f_r,
    c0_s, c0_r, c1_s, c1_r, c2_s, c2_r, wc_s, wc_r, wi_s, wi_r, wk_s, wk_r, wj_s, wj_r, o_s, o_r,
):
    q = lax.axis_index("queue")
    t = lax.axis_index("tok")
    core = lax.rem(q, 2)
    zlo = lax.rem(q // 2, 2)
    col = q // 4
    inner_q = q + 2 - 4 * zlo
    inner = (inner_q, t)
    cut = (inner_q, 1 - t)
    peer = (q, 1 - t)
    other = (q + 1 - 2 * core, t)
    upper = (q + 4, t)
    lower = (q - 4, t)
    has_up, has_low = col < COLS - 1, col > 0
    pending = []

    def send(src, dst, s_sem, r_sem, to, when=None):
        copy = pltpu.make_async_remote_copy(
            src_ref=src, dst_ref=dst, send_sem=s_sem, recv_sem=r_sem, device_id=to, device_id_type=MESH
        )
        pending.append((copy, when))
        if when is None:
            copy.start()
        else:
            pl.when(when)(copy.start)

    def recv(dst, s_sem, r_sem, to, when=None):
        copy = pltpu.make_async_remote_copy(
            src_ref=dst, dst_ref=dst, send_sem=s_sem, recv_sem=r_sem, device_id=to, device_id_type=MESH
        )
        if when is None:
            copy.wait_recv()
        else:
            pl.when(when)(copy.wait_recv)

    loads = [
        pltpu.make_async_copy(w_hbm.at[i], w_v.at[i], w_sem.at[i]) for i in range(3)
    ]
    loads[1].start()
    loads[2].start()
    wo_load = pltpu.make_async_copy(
        wo_hbm, wo_v.at[pl.ds(pl.multiple_of(t * 768, 768), 768)], w_sem.at[3]
    )

    barrier = pltpu.get_barrier_semaphore()
    for to in (inner, cut, peer, other):
        pl.semaphore_signal(barrier, inc=1, device_id=to, device_id_type=MESH)

    @pl.when(has_up)
    def _():
        pl.semaphore_signal(barrier, inc=1, device_id=upper, device_id_type=MESH)

    @pl.when(has_low)
    def _():
        pl.semaphore_signal(barrier, inc=1, device_id=lower, device_id_type=MESH)

    def normalize(r):
        rows = pl.ds(r * 128, 128)
        x = x_ref[0, rows, :].astype(jnp.float32)
        inv = lax.rsqrt(jnp.mean(x * x, axis=-1, keepdims=True) + EPS)
        nrm[0, rows, :] = (x * inv * (1.0 + mod_ref[1:2, :]) + mod_ref[0:1, :]).astype(jnp.bfloat16)

    def send_normed(r):
        rows = pl.ds(r * 128, 128)
        send(nrm.at[0, rows], nrm.at[1, rows], cut_s.at[r], cut_r.at[r], cut)

    normalize(0)
    pl.semaphore_wait(barrier, 4 + jnp.where(has_up, 1, 0) + jnp.where(has_low, 1, 0))
    send_normed(0)
    normalize(1)
    first_normed = pending.pop()[0]
    send(off_ref, offs, off_sem.at[0], off_sem.at[1], inner)

    slot_of = {A: zlo, B: 1 - zlo, C1: 1 - zlo, D1: zlo, C2: 1 - zlo, D2: zlo}
    group_of = {A: 0, B: 1, C1: 2, D1: 3, C2: 2, D2: 3}
    rows_of = {
        A: pl.ds(0, 256), B: pl.ds(0, 256), C1: pl.ds(0, 128), D1: pl.ds(0, 128),
        C2: pl.ds(128, 128), D2: pl.ds(128, 128),
    }

    def frame(piece, of_core=core):
        return of_core + 2 * slot_of[piece]

    def near_at(side, piece, of_core=core):
        ref = near_a if piece in (A, B) else near_c
        return ref.at[side, frame(piece, of_core), :, rows_of[piece], :]

    def far_at(side, piece, of_core=core):
        ref = far_a if piece in (A, B) else far_c
        return ref.at[side, frame(piece, of_core), :, rows_of[piece], :]

    def q_at(piece):
        return qb.at[group_of[piece], rows_of[piece], :]

    def project(part, nslot, src0, rows, piece):
        st_rows = pl.ds((0, 256, 384)[part], rows)
        own = far_a if part == 0 else far_c
        there = (B, D1, D2)[part]
        for mat in (1, 2, 0):
            if part == 0:
                loads[mat].wait()
                if mat == 1:
                    loads[0].start()
            y = jnp.dot(
                nrm[nslot, src0 : src0 + rows, :], w_v[mat], preferred_element_type=jnp.float32
            )
            thirds = []
            for h in range(6):
                yh = y[:, h * DH : (h + 1) * DH]
                if mat != 2:
                    yh = yh * lax.rsqrt(jnp.mean(yh * yh, axis=-1, keepdims=True) + EPS)
                if mat == 0:
                    yh = yh * hs_ref[h] * (DH ** -0.5)
                thirds.append(yh.astype(jnp.bfloat16))
            for h in range(3):
                lanes = slice(h * DH, (h + 1) * DH)
                mine = jnp.where(zlo == 0, thirds[h], thirds[h + 3])
                theirs = jnp.where(zlo == 0, thirds[h + 3], thirds[h])
                if mat == 0:
                    qb[group_of[piece], rows_of[piece], lanes] = mine
                    st_q[st_rows, lanes] = theirs
                else:
                    own[0, frame(piece), mat - 1, rows_of[piece], lanes] = mine
                    st_kv[mat - 1, st_rows, lanes] = theirs
            if mat == 2:
                send(st_kv.at[:, st_rows], far_at(0, piece), inkv_s.at[part], inkv_r.at[part], inner)
                spread(piece)
            if mat == 0:
                send(st_q.at[st_rows], q_at(there), inq_s.at[part], inq_r.at[part], inner)

    def spread(piece):
        send(far_at(0, piece), near_at(1, piece), y_s.at[UP, piece], y_r.at[UP, piece], upper, has_up)
        send(far_at(0, piece), near_at(0, piece), y_s.at[DOWN, piece], y_r.at[DOWN, piece], lower, has_low)
        send(far_at(0, piece), far_at(0, piece), c0_s.at[piece], c0_r.at[piece], other)

    def from_inner(part, piece):
        recv(far_at(0, piece), inkv_s.at[part], inkv_r.at[part], inner)
        spread(piece)

    def pass_on(piece):
        recv(near_at(1, piece), y_s.at[UP, piece], y_r.at[UP, piece], upper, has_low)
        send(
            near_at(1, piece), far_at(2, piece), f_s.at[UP, piece], f_r.at[UP, piece], upper,
            has_up & has_low & (frame(piece) >= 1),
        )
        send(near_at(1, piece), near_at(1, piece), c1_s.at[UP, piece], c1_r.at[UP, piece], other, has_low)
        recv(near_at(0, piece), y_s.at[DOWN, piece], y_r.at[DOWN, piece], lower, has_up)
        send(
            near_at(0, piece), far_at(1, piece), f_s.at[DOWN, piece], f_r.at[DOWN, piece], lower,
            has_up & has_low & (frame(piece) <= 2),
        )
        send(near_at(0, piece), near_at(0, piece), c1_s.at[DOWN, piece], c1_r.at[DOWN, piece], other, has_up)

    from_up2, from_low2 = col < COLS - 2, col > 1

    def share_far(piece):
        when = from_low2 & (frame(piece) >= 1)
        recv(far_at(2, piece), f_s.at[UP, piece], f_r.at[UP, piece], upper, when)
        send(far_at(2, piece), far_at(2, piece), c2_s.at[UP, piece], c2_r.at[UP, piece], other, when)
        when = from_up2 & (frame(piece) <= 2)
        recv(far_at(1, piece), f_s.at[DOWN, piece], f_r.at[DOWN, piece], lower, when)
        send(far_at(1, piece), far_at(1, piece), c2_s.at[DOWN, piece], c2_r.at[DOWN, piece], other, when)

    j = core + 2 * zlo
    w_rows = 192 // WSUB

    def quarter(half, which, sub):
        return pl.ds(pl.multiple_of(half * 768 + which * 192 + sub * w_rows, 16), w_rows)

    other_j, inner_j = j + 1 - 2 * core, j + 2 - 4 * zlo
    diag_j = 3 - j

    def wo_cut(sub):
        src = pl.ds(pl.multiple_of(inner_j * 192 + sub * w_rows, 16), w_rows)
        send(wo_hbm.at[src], wo_v.at[quarter(t, inner_j, sub)], wc_s.at[sub], wc_r.at[sub], cut)

    def wo_share(sub):
        mine = wo_v.at[quarter(1 - t, j, sub)]
        recv(mine, wc_s.at[sub], wc_r.at[sub], cut)
        send(mine, mine, wi_s.at[sub], wi_r.at[sub], inner)
        send(mine, mine, wk_s.at[sub], wk_r.at[sub], other)

    def wo_second(sub):
        theirs = wo_v.at[quarter(1 - t, inner_j, sub)]
        recv(theirs, wi_s.at[sub], wi_r.at[sub], inner)
        send(theirs, theirs, wj_s.at[sub], wj_r.at[sub], other)

    def wo_last(sub):
        recv(wo_v.at[quarter(1 - t, other_j, sub)], wk_s.at[sub], wk_r.at[sub], other)
        recv(wo_v.at[quarter(1 - t, diag_j, sub)], wj_s.at[sub], wj_r.at[sub], other)

    project(0, 0, 0, 256, A)
    first_normed.wait_send()
    send_normed(1)
    wo_load.start()

    @pl.when(col == COLS - 1)
    def _():
        near_a[0] = jnp.zeros_like(near_a[0])
        near_c[0] = jnp.zeros_like(near_c[0])

    @pl.when(col == 0)
    def _():
        near_a[1] = jnp.zeros_like(near_a[1])
        near_c[1] = jnp.zeros_like(near_c[1])

    @pl.when(col >= COLS - 2)
    def _():
        far_a[1] = jnp.zeros_like(far_a[1])
        far_c[1] = jnp.zeros_like(far_c[1])

    @pl.when(col <= 1)
    def _():
        far_a[2] = jnp.zeros_like(far_a[2])
        far_c[2] = jnp.zeros_like(far_c[2])

    def place_of(unit):
        group, h = unit // 3, lax.rem(unit, 3)
        slot = jnp.where((group == 0) | (group == 3), zlo, 1 - zlo)
        return group, slot, pl.ds(pl.multiple_of(h * DH, DH), DH)

    def near_blocks(slot, ref, own):
        mine = core + 2 * slot
        o = jnp.where(slot == zlo, off_ref[0], offs[0])
        blocks = [(own, (0, mine), None)]
        for i in range(4):
            below = 4 + i - mine > WIN - 1 - o
            side = jnp.where(below, 1, 0)
            blocks.append((ref, (side, i), jnp.where(below, has_low, has_up)))
        return blocks

    def far_blocks(slot, ref):
        mine = core + 2 * slot
        o = jnp.where(slot == zlo, off_ref[0], offs[0])
        blocks = []
        for n in range(3):
            r = n + jnp.where(n >= mine, 1, 0)
            less = r < mine
            inside = jnp.where(less, mine - r <= o, r - mine <= WIN - 1 - o)
            side = jnp.where(inside, 0, jnp.where(less, 1, 2))
            blocks.append((ref, (side, r), inside | jnp.where(less, from_up2, from_low2)))
        return blocks

    def stage_blocks(stage, slot):
        if stage == 0:
            return near_blocks(slot, near_a, far_a)
        if stage == 1:
            return far_blocks(slot, far_a)
        if stage == 2:
            return near_blocks(slot, near_c, far_c)
        return far_blocks(slot, far_c)

    COUNT = (5, 3, 5, 3)

    def score(stage, unit, b, buf, top):
        group, slot, lanes = place_of(unit)
        ref, lead, valid = stage_blocks(stage, slot)[b]
        s = lax.dot_general(
            qb[group, :, lanes], ref[(*lead, 0, slice(None), lanes)],
            (((1,), (1,)), ((), ())), preferred_element_type=jnp.float32,
        )
        buf[:, b * HALF : (b + 1) * HALF] = s
        high = jnp.maximum(s[:, :DH], s[:, DH:])
        if valid is not None:
            high = jnp.where(valid, high, LOW)
        return high if top is None else jnp.maximum(top, high)

    def peak(stage, unit, top):
        high = jnp.broadcast_to(jnp.max(top, axis=1, keepdims=True), (HALF, DH))
        if stage > 0:
            before = m_s[unit]
            high = jnp.maximum(high, before)
            scale = jnp.exp(before - high)
            acc_s[unit] = acc_s[unit] * scale
            l_s[unit] = l_s[unit] * scale
        m_s[unit] = high

    def weigh(stage, unit, b, buf, high, total, weighted):
        _, slot, lanes = place_of(unit)
        ref, lead, valid = stage_blocks(stage, slot)[b]
        base = high if valid is None else jnp.where(valid, high, HIGH)
        p = [jnp.exp(buf[:, b * HALF + c * DH : b * HALF + (c + 1) * DH] - base) for c in range(2)]
        part = p[0] + p[1]
        rounded = jnp.concatenate([c.astype(jnp.bfloat16) for c in p], axis=1)
        o = jnp.dot(rounded, ref[(*lead, 1, slice(None), lanes)], preferred_element_type=jnp.float32)
        return (part if total is None else total + part), (o if weighted is None else weighted + o)

    def finish(stage, unit, total, weighted):
        if stage > 0:
            total = total + l_s[unit]
            weighted = weighted + acc_s[unit]
        if stage < 3:
            l_s[unit] = total
            acc_s[unit] = weighted
        else:
            group, _, lanes = place_of(unit)
            ob[group, :, lanes] = (weighted / jnp.sum(total, axis=1, keepdims=True)).astype(jnp.bfloat16)

    def start_unit(stage, unit, buf):
        top = None
        for b in range(COUNT[stage]):
            top = score(stage, unit, b, buf, top)
        peak(stage, unit, top)

    def step(stage, unit, buf, following, other_buf):
        high = m_s[unit]
        top = total = weighted = None
        for b in range(COUNT[stage]):
            if following is not None:
                top = score(stage, following, b, other_buf, top)
            total, weighted = weigh(stage, unit, b, buf, high, total, weighted)
        finish(stage, unit, total, weighted)
        if following is not None:
            peak(stage, following, top)

    def units(stage, low, high):
        start_unit(stage, low, even)

        def two(i, carry):
            unit = low + 2 * i
            step(stage, unit, even, unit + 1, odd)
            step(stage, unit + 1, odd, jnp.minimum(unit + 2, high - 1), even)
            return carry

        lax.fori_loop(0, (high - low) // 2, two, 0)

    def near_from_core(*pieces):
        for piece in pieces:
            recv(near_at(1, piece, 1 - core), c1_s.at[UP, piece], c1_r.at[UP, piece], other, has_low)
            recv(near_at(0, piece, 1 - core), c1_s.at[DOWN, piece], c1_r.at[DOWN, piece], other, has_up)

    def own_from_core(*pieces):
        for piece in pieces:
            recv(far_at(0, piece, 1 - core), c0_s.at[piece], c0_r.at[piece], other)

    def far_from_core(*pieces):
        for piece in pieces:
            recv(
                far_at(2, piece, 1 - core), c2_s.at[UP, piece], c2_r.at[UP, piece], other,
                from_low2 & (frame(piece, 1 - core) >= 1),
            )
            recv(
                far_at(1, piece, 1 - core), c2_s.at[DOWN, piece], c2_r.at[DOWN, piece], other,
                from_up2 & (frame(piece, 1 - core) <= 2),
            )

    from_inner(0, B)
    pass_on(A)
    recv(nrm.at[1, pl.ds(0, 128)], cut_s.at[0], cut_r.at[0], cut)
    project(1, 1, 0, 128, C1)
    pass_on(B)
    from_inner(1, D1)
    recv(offs, off_sem.at[0], off_sem.at[1], inner)
    recv(q_at(B), inq_s.at[0], inq_r.at[0], inner)
    near_from_core(A, B)
    own_from_core(A, B)
    units(0, 0, 6)
    recv(nrm.at[1, pl.ds(128, 128)], cut_s.at[1], cut_r.at[1], cut)
    wo_cut(0)
    wo_cut(1)
    project(2, 1, 128, 128, C2)
    from_inner(2, D2)
    wo_cut(2)
    wo_cut(3)
    recv(q_at(D1), inq_s.at[1], inq_r.at[1], inner)
    recv(q_at(D2), inq_s.at[2], inq_r.at[2], inner)
    units(0, 6, 12)
    wo_share(0)
    wo_share(1)
    pass_on(C1)
    pass_on(D1)
    pass_on(C2)
    share_far(A)
    share_far(B)
    far_from_core(A, B)
    units(1, 0, 6)
    pass_on(D2)
    wo_share(2)
    wo_share(3)
    units(1, 6, 12)
    share_far(C1)
    share_far(D1)
    near_from_core(C1, D1, C2, D2)
    own_from_core(C1, D1, C2, D2)
    units(2, 0, 6)
    wo_second(0)
    wo_second(1)
    units(2, 6, 12)
    share_far(C2)
    share_far(D2)
    far_from_core(C1, D1, C2, D2)

    triple = 2 * t + zlo
    goes_to = (None, inner, cut, peer)
    order = (3, 4, 5, 6, 7, 8, 9, 10, 11, 0, 1, 2)
    start_unit(3, order[0], even)
    for n, unit in enumerate(order):
        bufs = (even, odd) if n % 2 == 0 else (odd, even)
        step(3, unit, bufs[0], order[n + 1] if n < 11 else None, bufs[1])
        group = unit // 3
        if unit % 3 == 2 and group > 0:
            send(ob.at[group], att.at[triple], o_s.at[group - 1], o_r.at[group - 1], goes_to[group])
    att[triple] = ob[0]
    wo_second(2)
    wo_second(3)

    def joined(half):
        return jnp.concatenate([att[2 * half], att[2 * half + 1]], axis=1)

    def out_rows(half):
        return pl.ds(pl.multiple_of(half * 768, 768), 768)

    wo_load.wait()
    recv(att.at[2 * t + 1 - zlo], o_s.at[0], o_r.at[0], inner)
    left = joined(t)
    for n in range(D // 512):
        buf, at = (even, n * 512) if n < 3 else (odd, (n - 3) * 512)
        buf[:, at : at + 512] = jnp.dot(
            left, wo_v[out_rows(t), n * 512 : (n + 1) * 512], preferred_element_type=jnp.float32
        )
    for sub in range(WSUB):
        wo_last(sub)
    recv(att.at[2 * (1 - t) + 1 - zlo], o_s.at[1], o_r.at[1], cut)
    recv(att.at[2 * (1 - t) + zlo], o_s.at[2], o_r.at[2], peer)
    right = joined(1 - t)
    for n in range(D // 512):
        buf, at = (even, n * 512) if n < 3 else (odd, (n - 3) * 512)
        lanes = slice(n * 512, (n + 1) * 512)
        branch = buf[:, at : at + 512] + jnp.dot(
            right, wo_v[out_rows(1 - t), lanes], preferred_element_type=jnp.float32
        )
        x = x_ref[0, :, lanes].astype(jnp.float32)
        out_ref[0, :, lanes] = (x + mod_ref[2:3, lanes] * branch).astype(jnp.bfloat16)
    for copy, when in pending:
        if when is None:
            copy.wait_send()
        else:
            pl.when(when)(copy.wait_send)


def shards(latents, levels, offsets, level_table, w_qkv, w_out, head_scale):
    table = jnp.transpose(level_table, (1, 0, 2))
    modulation = lax.dynamic_index_in_dim(table, levels[0], 1, keepdims=False)
    weights = jnp.transpose(w_qkv, (1, 0, 2))
    bf, f32 = jnp.bfloat16, jnp.float32
    dma = pltpu.SemaphoreType.DMA
    vmem = pl.BlockSpec(memory_space=pltpu.VMEM)
    smem = pl.BlockSpec(memory_space=pltpu.SMEM)
    hbm = pl.BlockSpec(memory_space=pl.ANY)
    pair = lambda *n: [dma(n), dma(n)]
    return pl.pallas_call(
        body,
        out_shape=jax.ShapeDtypeStruct((1, HALF, D), bf),
        in_specs=[vmem, vmem, hbm, hbm, smem, smem],
        out_specs=vmem,
        scratch_shapes=[
            pltpu.VMEM((2, 4, 2, HALF, TRI), bf),
            pltpu.VMEM((2, 4, 2, HALF, TRI), bf),
            pltpu.VMEM((3, 4, 2, HALF, TRI), bf),
            pltpu.VMEM((3, 4, 2, HALF, TRI), bf),
            pltpu.VMEM((4, HALF, TRI), bf),
            pltpu.VMEM((3, D, 768), bf),
            pltpu.VMEM((1536, D), bf),
            pltpu.VMEM((2, HALF, D), bf),
            pltpu.VMEM((2, TOK, TRI), bf),
            pltpu.VMEM((TOK, TRI), bf),
            pltpu.VMEM((HALF, D // 2), f32),
            pltpu.VMEM((HALF, D // 2), f32),
            pltpu.VMEM((12, HALF, DH), f32),
            pltpu.VMEM((12, HALF, DH), f32),
            pltpu.VMEM((12, HALF, DH), f32),
            pltpu.VMEM((4, HALF, TRI), bf),
            pltpu.VMEM((4, HALF, TRI), bf),
            pltpu.SMEM((1,), jnp.int32),
            dma((4,)), dma((2,)),
            *pair(2), *pair(3), *pair(3), *pair(2, 6), *pair(2, 6),
            *pair(6), *pair(2, 6), *pair(2, 6),
            *pair(WSUB), *pair(WSUB), *pair(WSUB), *pair(WSUB), *pair(3),
        ],
        compiler_params=pltpu.CompilerParams(
            collective_id=0, has_side_effects=True, vmem_limit_bytes=62 * 2**20
        ),
        cost_estimate=pl.CostEstimate(flops=17 * 10**9, bytes_accessed=25 * 10**6, transcendentals=13 * 10**6),
        name="frame_attention",
    )(latents, modulation, weights, w_out, offsets, head_scale)


def solution(mesh):
    placed = (
        P("queue", "tok", None),
        P("queue"),
        P("queue"),
        P(),
        P(None, None, "tok"),
        P("tok", None),
        P("tok"),
    )
    return jax.shard_map(
        shards, mesh=mesh, in_specs=placed, out_specs=P("queue", "tok", None), check_vma=False
    )
```
